128 devices in a mesh: group: 8 (over y, core), expert: 4 (over z), tp: 4 (over x).
Axes of the slice: x: 4, y: 4, z: 4, core: 2. Of those that a mesh axis runs over, the one named last changes fastest.
Arguments:
- tokens: bfloat16 [4096, 5120], P(('group', 'expert'), 'tp'), may hold values from -6 to 6
- cotangent: bfloat16 [4096, 5120], P(('group', 'expert'), 'tp'), may hold values from -3 to 3
- group_logits: float32 [4096, 8], P(('group', 'expert')), may hold values from -1 to 301
- expert_logits: float32 [4096, 32], P(('group', 'expert')), may hold values from -1 to 301
- expert_ids: int32 [4096, 6], P(('group', 'expert')), may hold values from 0 to 31, as said below
- w_gate: bfloat16 [32, 5120, 1536], P(('group', 'expert'), None, 'tp'), may hold values from -0.078125 to 0.078125
- w_up: bfloat16 [32, 5120, 1536], P(('group', 'expert'), None, 'tp'), may hold values from -0.078125 to 0.078125
- w_down: bfloat16 [32, 1536, 5120], P(('group', 'expert'), 'tp'), may hold values from -0.15625 to 0.15625
Outputs:
- mixed: bfloat16 [4096, 5120], P(('group', 'expert'), 'tp')
- d_tokens: bfloat16 [4096, 5120], P(('group', 'expert'), 'tp')
- d_group_logits: float32 [4096, 8], P(('group', 'expert'))
- d_expert_logits: float32 [4096, 32], P(('group', 'expert'))
- d_w_gate: bfloat16 [32, 5120, 1536], P(('group', 'expert'), None, 'tp')
- d_w_up: bfloat16 [32, 5120, 1536], P(('group', 'expert'), None, 'tp')
- d_w_down: bfloat16 [32, 1536, 5120], P(('group', 'expert'), 'tp')
The draws below stay inside these ranges and needn't reach their ends.
Inputs may be any that keep to these rules, and one draw needn't show every extreme that they name: `expert_ids`: A token names 6 different experts. Of the 128 tokens of one index of group and expert (aligned blocks of rows), no expert is named by more than 26, and one expert, the same for every block, is named by exactly 26.
All inputs are finite; a program needn't handle non-finite values.
Results may differ from the reference program's by a relative error of at most 0.015.
Values may be sent and summed in bfloat16 or wider, within the bound.
No kernel may reach another device: no remote copies, remote signals or barrier semaphores. Data moves between devices by JAX's collectives and lax.ppermute only.
A program may use at most 192 MiB of HBM per device.

```python
import jax
import jax.numpy as jnp
from jax import lax

D = 5120
FF = 1536
TOPK = 6
TOK_DEV = 128
NGROUPS = 8
EXPERTS = 32
CAP = 26
TOKENS = 4096
N_GROUP = 8
N_EXPERT = 4
N_TP = 4


def draw_group_logits(key, part):
    key = jax.random.fold_in(key, 31)
    first = jax.random.fold_in(key, 0)
    values = 0.2 * jax.random.truncated_normal(first, -4.0, 4.0, (TOKENS, NGROUPS), jnp.float32)
    return values


def draw_expert_logits(key, part):
    key = jax.random.fold_in(key, 47)
    first = jax.random.fold_in(key, 0)
    values = 0.2 * jax.random.truncated_normal(first, -4.0, 4.0, (TOKENS, EXPERTS), jnp.float32)
    return values


def draw_expert_ids(key, part):
    key = jax.random.fold_in(key, 7)
    block_count = TOKENS // TOK_DEV
    pick_total = TOK_DEV * TOPK
    slack = EXPERTS * CAP - pick_total
    others = EXPERTS - 1
    key_full, key_blocks = jax.random.split(key)
    full_expert = jax.random.randint(key_full, (), 0, EXPERTS)

    def one_block(block_key):
        key_order, key_rows, key_cols = jax.random.split(block_key, 3)
        scores = jax.random.permutation(key_order, EXPERTS)
        scores = jnp.where(jnp.arange(EXPERTS) == full_expert, -1, scores)
        order = jnp.argsort(scores).astype(jnp.int32)
        ranks = jnp.arange(EXPERTS)
        fewer = slack // others + (ranks - 1 < slack % others).astype(jnp.int32)
        fewer = jnp.where(ranks == 0, 0, fewer)
        loads = CAP - fewer
        ends = jnp.cumsum(loads)
        index = jnp.arange(pick_total)
        position = jnp.sum((ends[None, :] <= index[:, None]).astype(jnp.int32), 1)
        chosen = order[position].reshape(TOPK, TOK_DEV).T
        shuffle = jax.random.permutation(key_rows, TOK_DEV)
        chosen = chosen[shuffle]
        columns = jax.vmap(lambda row_key: jax.random.permutation(row_key, TOPK))(jax.random.split(key_cols, TOK_DEV))
        return jnp.take_along_axis(chosen, columns, 1)
    chosen_all = jax.vmap(one_block)(jax.random.split(key_blocks, block_count))
    return chosen_all.reshape(TOKENS, TOPK).astype(jnp.int32)


def shard_levels(own_key, shape, pieces, low, top_value):
    gain, own = 1.0, jax.random.fold_in(own_key, 6)
    for dim, blocks in pieces:
        steps = jnp.exp(jax.random.uniform(jax.random.fold_in(own, dim), (blocks,), jnp.float32, low / len(pieces), top_value / len(pieces)))
        gain = gain * jnp.repeat(steps, shape[dim] // blocks).reshape([-1 if axis == dim else 1 for axis in range(len(shape))])
    return gain


def normal_values(own_key, dims, scale, limit, cuts=(), kind=jnp.bfloat16):
    result = scale * jax.random.normal(own_key, dims, jnp.float32)
    if cuts:
        result = result * shard_levels(own_key, dims, cuts, -0.22, 0.18)
    return jnp.clip(result, -limit, limit).astype(kind)


def setup_inputs(seed: int = 0) -> dict:
    splits = jax.random.split(jax.random.key(seed), 9)
    tokens = normal_values(splits[0], (TOKENS, D), 1.0, 6.0, ((0, 32), (1, 4)))
    cotangent = normal_values(splits[1], (TOKENS, D), 0.5, 3.0, ((0, 32), (1, 4)))
    group_logits = draw_group_logits(jax.random.fold_in(splits[8], 71), 0)
    expert_logits = draw_expert_logits(jax.random.fold_in(splits[8], 71), 0)
    expert_ids = draw_expert_ids(jax.random.fold_in(splits[8], 71), 0)
    w_gate = normal_values(splits[5], (EXPERTS, D, FF), D ** -0.5, 0.078125, ((0, 32), (2, 4)))
    w_up = normal_values(splits[6], (EXPERTS, D, FF), D ** -0.5, 0.078125, ((0, 32), (2, 4)))
    w_down = normal_values(splits[7], (EXPERTS, FF, D), FF ** -0.5, 0.15625, ((0, 32), (1, 4)))
    return dict(tokens=tokens, cotangent=cotangent, group_logits=group_logits, expert_logits=expert_logits, expert_ids=expert_ids, w_gate=w_gate, w_up=w_up, w_down=w_down)


route_scale = 16.0

def pick_gates(group_logits, expert_logits, expert_ids):
    row_count, group_count = group_logits.shape
    expert_count = expert_logits.shape[1]
    per_group = expert_count // group_count
    group_probs = jax.nn.softmax(group_logits, axis=-1)
    inner_probs = jax.nn.softmax(expert_logits.reshape(row_count, group_count, per_group), axis=-1).reshape(row_count, expert_count)
    owner = expert_ids // per_group
    return route_scale * jnp.take_along_axis(group_probs, owner, 1) * jnp.take_along_axis(inner_probs, expert_ids, 1)

def reference(tokens, cotangent, group_logits, expert_logits, expert_ids, w_gate, w_up, w_down):
    gate_value = pick_gates(group_logits, expert_logits, expert_ids)
    gate_half = gate_value.astype(jnp.bfloat16)
    row_total = N_GROUP * N_EXPERT * CAP
    block_width = FF // N_TP
    flat_ids = expert_ids.reshape(-1)

    def expert_step(carry, inputs):
        mixed_sum, grad_sum, gate_grad = carry
        expert, w_first, w_second, w_third = inputs
        chosen = flat_ids == expert
        found = jnp.nonzero(chosen, size=row_total, fill_value=0)[0].astype(jnp.int32)
        valid = jnp.arange(row_total) < jnp.sum(chosen.astype(jnp.int32))
        rows_tok = found // TOPK
        rows_pick = found % TOPK
        weight = jnp.where(valid, gate_half[rows_tok, rows_pick].astype(jnp.float32), jnp.float32(0.0))
        input_rows = jnp.where(valid[:, None], tokens[rows_tok], jnp.zeros((), jnp.bfloat16))
        back_rows = (weight[:, None] * cotangent[rows_tok].astype(jnp.float32)).astype(jnp.bfloat16)
        pre_gate = jnp.dot(input_rows, w_first, preferred_element_type=jnp.float32)
        pre_up = jnp.dot(input_rows, w_second, preferred_element_type=jnp.float32)
        sigmoid_gate = jax.nn.sigmoid(pre_gate)
        silu_gate = pre_gate * sigmoid_gate
        hidden = (silu_gate * pre_up).astype(jnp.bfloat16)
        out_acc = jnp.zeros((row_total, D), jnp.float32)
        for block in range(N_TP):
            lower = block * block_width
            term = jnp.dot(hidden[:, lower:lower + block_width], w_third[lower:lower + block_width], preferred_element_type=jnp.float32)
            out_acc = out_acc + lax.optimization_barrier(term.astype(jnp.bfloat16)).astype(jnp.float32)
        out_rows = out_acc.astype(jnp.bfloat16)
        mixed_sum = mixed_sum.at[rows_tok].add(weight[:, None] * out_rows.astype(jnp.float32))
        dots = lax.optimization_barrier(jnp.sum(cotangent[rows_tok].astype(jnp.float32) * out_rows.astype(jnp.float32), 1))
        gate_grad = gate_grad.at[rows_tok, rows_pick].add(jnp.where(valid, dots, jnp.float32(0.0)))
        grad_hidden = jnp.dot(back_rows, w_third.T, preferred_element_type=jnp.float32)
        grad_gate = (grad_hidden * pre_up * sigmoid_gate * (1.0 + pre_gate * (1.0 - sigmoid_gate))).astype(jnp.bfloat16)
        grad_up = (grad_hidden * silu_gate).astype(jnp.bfloat16)
        grad_acc = jnp.zeros((row_total, D), jnp.float32)
        for block in range(N_TP):
            lower = block * block_width
            term = jnp.dot(grad_gate[:, lower:lower + block_width], w_first[:, lower:lower + block_width].T, preferred_element_type=jnp.float32)
            term = term + jnp.dot(grad_up[:, lower:lower + block_width], w_second[:, lower:lower + block_width].T, preferred_element_type=jnp.float32)
            grad_acc = grad_acc + lax.optimization_barrier(term.astype(jnp.bfloat16)).astype(jnp.float32)
        grad_rows = grad_acc.astype(jnp.bfloat16)
        grad_sum = grad_sum.at[rows_tok].add(jnp.where(valid[:, None], grad_rows.astype(jnp.float32), jnp.float32(0.0)))
        grad_first = jnp.dot(input_rows.T, grad_gate, preferred_element_type=jnp.float32).astype(jnp.bfloat16)
        grad_second = jnp.dot(input_rows.T, grad_up, preferred_element_type=jnp.float32).astype(jnp.bfloat16)
        grad_third = jnp.dot(hidden.T, back_rows, preferred_element_type=jnp.float32).astype(jnp.bfloat16)
        return ((mixed_sum, grad_sum, gate_grad), (grad_first, grad_second, grad_third))
    start = (jnp.zeros((TOKENS, D), jnp.float32), jnp.zeros((TOKENS, D), jnp.float32), jnp.zeros((TOKENS, TOPK), jnp.float32))
    numbers = jnp.arange(EXPERTS, dtype=jnp.int32)
    (mixed_sum, grad_sum, gate_grad), (grad_first, grad_second, grad_third) = lax.scan(expert_step, start, (numbers, w_gate, w_up, w_down))

    def gate_of(group_part, expert_part):
        return pick_gates(group_part, expert_part, expert_ids)
    unused, pull_back = jax.vjp(gate_of, group_logits, expert_logits)
    group_grad, logit_grad = pull_back(gate_grad)
    return (mixed_sum.astype(jnp.bfloat16), grad_sum.astype(jnp.bfloat16), group_grad, logit_grad, grad_first, grad_second, grad_third)
```

```python
import jax
import jax.numpy as jnp
from jax import lax
from jax.sharding import PartitionSpec as P

route_scale = 16.0
both = ("group", "expert")
bf16 = jnp.bfloat16
f32 = jnp.float32


def dot(left, right, dims=((1,), (0,))):
    return lax.dot_general(left, right, (dims, ((), ())), preferred_element_type=f32)


def up(value):
    return lax.ppermute(value, "tp", [(i, (i + 1) % 4) for i in range(4)])


def down(value):
    return lax.ppermute(value, "tp", [(i, (i + 3) % 4) for i in range(4)])


def across(value):
    return lax.ppermute(value, "tp", [(i, (i + 2) % 4) for i in range(4)])


def exchange(value):
    return lax.all_to_all(value, both, split_axis=0, concat_axis=0, tiled=True)


def route(group_logits, expert_logits, expert_ids, capacity):
    rows, groups = group_logits.shape
    experts = expert_logits.shape[1]
    per = experts // groups
    group_probs = jax.nn.softmax(group_logits.T, axis=0)
    inner = jax.nn.softmax(expert_logits.T.reshape(groups, per, rows), axis=1)
    gate = route_scale * group_probs[:, None, :] * inner
    ids = expert_ids.T
    numbers = jnp.arange(experts, dtype=jnp.int32)
    chosen = jnp.any(ids[:, None, :] == numbers[None, :, None], axis=0)
    earlier = jnp.arange(rows)[:, None] < jnp.arange(rows)[None, :]
    rank = dot(chosen.astype(bf16), earlier.astype(bf16))
    code = jnp.where(chosen, rank, -1.0).astype(bf16)
    slots = experts * capacity
    spread = (jnp.arange(slots)[:, None] // capacity == numbers[None, :]).astype(bf16)
    place = (jnp.arange(slots) % capacity).astype(f32)[:, None]
    pick = dot(spread, code) == place
    gate_half = gate.astype(bf16).reshape(experts, rows)
    slot_gate = jnp.sum(jnp.where(pick, dot(spread, gate_half), 0.0), axis=1)
    return group_probs, inner, pick.astype(bf16), spread, slot_gate


def body(tokens, cotangent, group_logits, expert_logits, expert_ids, w_gate, w_up, w_down):
    rows, width = tokens.shape
    experts = expert_logits.shape[1]
    groups = group_logits.shape[1]
    capacity = min(rows, (rows * expert_ids.shape[1] + experts - 1) // experts + 2)
    slots = experts * capacity
    half = slots // 2
    w_gate, w_up, w_down = w_gate[0], w_up[0], w_down[0]
    units = w_down.shape[0]
    me = lax.axis_index("tp")
    far, right, left = (me + 2) % 4, (me + 1) % 4, (me + 3) % 4

    def columns(owner):
        return lax.dynamic_slice(w_down, (0, owner * width), (units, width))

    down_own = columns(me)
    down_left = up(columns(right))
    down_right = down(columns(left))
    down_far = across(columns(far))

    group_probs, inner, pick, spread, slot_gate = route(
        group_logits, expert_logits, expert_ids, capacity
    )
    tok = exchange(dot(pick, tokens).astype(bf16).reshape(experts, capacity, width))
    tok = tok.reshape(slots, width)
    cot = exchange(dot(pick, cotangent).astype(bf16).reshape(experts, capacity, width))
    cot = cot.reshape(slots, width)
    gate = exchange(slot_gate.reshape(experts, capacity)).reshape(slots, 1)

    tok_left = up(tok)
    tok_right = down(tok)
    tok_far = jnp.concatenate([up(tok_left[:half]), down(tok_right[half:])], axis=0)
    pieces = ((tok, me), (tok_left, left), (tok_right, right), (tok_far, far))

    def rows_of(weight, owner):
        return lax.dynamic_slice(weight, (owner * width, 0), (width, units))

    pre_gate = sum(dot(part, rows_of(w_gate, owner)) for part, owner in pieces)
    pre_up = sum(dot(part, rows_of(w_up, owner)) for part, owner in pieces)

    last = ((1,), (1,))
    part_left = dot(cot, down_left, last).astype(bf16)
    part_right = dot(cot, down_right, last).astype(bf16)
    part_far = dot(cot, down_far, last).astype(bf16)
    back = dot(cot, down_own, last)
    back = back + down(part_left).astype(f32) + up(part_right).astype(f32) + across(part_far).astype(f32)

    sig = jax.nn.sigmoid(pre_gate)
    silu = pre_gate * sig
    hidden = silu * pre_up
    gate_grad = jnp.sum(hidden * back, axis=1)
    weighted = (hidden * gate).astype(bf16)
    back = back * gate
    grad_gate = (back * pre_up * sig * (1.0 + pre_gate * (1.0 - sig))).astype(bf16)
    grad_up = (back * silu).astype(bf16)

    hid_left = up(weighted)
    hid_right = down(weighted)
    hid_far = jnp.concatenate([up(hid_left[:half]), down(hid_right[half:])], axis=0)
    hids = (weighted, hid_left, hid_right, hid_far)
    downs = (down_own, down_left, down_right, down_far)
    out = sum(dot(h, d) for h, d in zip(hids, downs)).astype(bf16)
    out = exchange(out.reshape(experts, capacity, width)).reshape(slots, width)
    first = ((0,), (0,))
    mixed = dot(pick, out, first).astype(bf16)

    def grad_part(owner, lo, size):
        at = owner * width + lo
        return dot(grad_gate, lax.dynamic_slice(w_gate, (at, 0), (size, units)), last) + dot(
            grad_up, lax.dynamic_slice(w_up, (at, 0), (size, units)), last
        )

    token_grads = []
    for lo in (0, width // 2):
        size = width // 2
        part = grad_part(far, lo, size).astype(bf16)
        from_left, from_right = up(part[:half]), down(part[half:])
        part = grad_part(right, lo, size)
        part = jnp.concatenate([part[:half] + from_left.astype(f32), part[half:]], axis=0)
        from_left = up(part.astype(bf16))
        part = grad_part(left, lo, size)
        part = jnp.concatenate([part[:half], part[half:] + from_right.astype(f32)], axis=0)
        from_right = down(part.astype(bf16))
        total = grad_part(me, lo, size) + from_left.astype(f32) + from_right.astype(f32)
        total = exchange(total.astype(bf16).reshape(experts, capacity, size)).reshape(slots, size)
        token_grads.append(dot(pick, total, first).astype(bf16))
    token_grad = jnp.concatenate(token_grads, axis=1)

    d_gate = jnp.zeros(w_gate.shape, bf16)
    d_up = jnp.zeros(w_up.shape, bf16)
    for part, owner in pieces:
        at = (owner * width, 0)
        d_gate = lax.dynamic_update_slice(d_gate, dot(part, grad_gate, first).astype(bf16), at)
        d_up = lax.dynamic_update_slice(d_up, dot(part, grad_up, first).astype(bf16), at)

    blocks = [dot(h, cot, first).astype(bf16) for h in hids]
    d_down = jnp.zeros(w_down.shape, bf16)
    for block, owner in (
        (blocks[0], me),
        (down(blocks[1]), right),
        (up(blocks[2]), left),
        (across(blocks[3]), far),
    ):
        d_down = lax.dynamic_update_slice(d_down, block, (0, owner * width))

    gate_grad = exchange(gate_grad.reshape(experts, capacity)).reshape(slots, 1)
    dense = lax.dot_general(
        spread.astype(f32) * gate_grad, pick.astype(f32), (first, ((), ())),
        precision=lax.Precision.HIGHEST, preferred_element_type=f32,
    )
    dense = lax.psum(dense, "tp").reshape(groups, experts // groups, rows)
    scaled = route_scale * dense * inner
    group_part = jnp.sum(scaled, axis=1)
    group_grad = group_probs * (group_part - jnp.sum(group_probs * group_part, axis=0, keepdims=True))
    logit_grad = group_probs[:, None, :] * (scaled - inner * group_part[:, None, :])
    return (
        mixed,
        token_grad,
        group_grad.T,
        logit_grad.reshape(experts, rows).T,
        d_gate[None],
        d_up[None],
        d_down[None],
    )


def solution(mesh):
    rows = P(both, "tp")
    router = P(both, None)
    wide = P(both, None, "tp")
    tall = P(both, "tp", None)
    return jax.shard_map(
        body,
        mesh=mesh,
        in_specs=(rows, rows, router, router, router, wide, wide, tall),
        out_specs=(rows, rows, router, router, wide, wide, tall),
        check_vma=False,
    )
```

```python
import jax
import jax.numpy as jnp
from jax import lax
from jax.experimental import pallas as pl
from jax.experimental.pallas import tpu as pltpu
from jax.sharding import PartitionSpec as P

route_scale = 16.0
both = ("group", "expert")
bf16 = jnp.bfloat16
f32 = jnp.float32


def dot(left, right, dims=((1,), (0,))):
    return lax.dot_general(left, right, (dims, ((), ())), preferred_element_type=f32)


def up(value):
    return lax.ppermute(value, "tp", [(i, (i + 1) % 4) for i in range(4)])


def down(value):
    return lax.ppermute(value, "tp", [(i, (i + 3) % 4) for i in range(4)])


def across(value):
    return lax.ppermute(value, "tp", [(i, (i + 2) % 4) for i in range(4)])


def tie(*values):
    return lax.optimization_barrier(values)


def exchange(value):
    return lax.all_to_all(value, both, split_axis=0, concat_axis=0, tiled=True)


light = pl.CostEstimate(flops=1, bytes_accessed=1, transcendentals=0)
outer = ((0,), (0,))


def up_weight_kernel(owner_ref, own, left, right, far, grad_ref, gate_ref, up_ref):
    step = pl.program_id(0)
    for number, part in enumerate((own, left, right, far)):

        @pl.when(step // 2 == number)
        def _():
            both_grads = dot(part[...], grad_ref[...], outer).astype(bf16)
            units = gate_ref.shape[1]
            gate_ref[...] = both_grads[:, :units]
            up_ref[...] = both_grads[:, units:]


def up_weight_grads(owners, parts, grads):
    slots, width = parts[0].shape
    units = grads.shape[1] // 2
    size = width // 2

    def part_spec(number):
        return pl.BlockSpec(
            (slots, size), lambda i, owner: (0, jnp.clip(i - 2 * number, 0, 1))
        )

    out_spec = pl.BlockSpec((size, units), lambda i, owner: (owner[i // 2] * 2 + i % 2, 0))
    shape = jax.ShapeDtypeStruct((4 * width, units), bf16)
    return pl.pallas_call(
        up_weight_kernel,
        grid_spec=pltpu.PrefetchScalarGridSpec(
            num_scalar_prefetch=1,
            grid=(8,),
            in_specs=[part_spec(n) for n in range(4)]
            + [pl.BlockSpec((slots, 2 * units), lambda i, owner: (0, 0))],
            out_specs=[out_spec, out_spec],
        ),
        out_shape=[shape, shape],
        cost_estimate=light,
        compiler_params=pltpu.CompilerParams(vmem_limit_bytes=40 << 20),
        name="up_weight_grads",
    )(owners, *parts, grads)


def down_weight_kernel(owner_ref, hid_ref, own, left, right, far, ahead, out_ref):
    step = pl.program_id(0)
    for number, part in enumerate((own, left, right, far, ahead)):

        @pl.when(jnp.minimum(step, 4) == number)
        def _():
            out_ref[...] = dot(hid_ref[...], part[...], outer).astype(bf16)


def down_weight_grads(owners, hid, parts):
    slots, units = hid.shape
    size = parts[0].shape[1]
    whole = pl.BlockSpec((slots, size), lambda i, owner: (0, 0))

    def out_block(i, owner):
        return 0, owner[i % 4] * 2 + i // 4

    return pl.pallas_call(
        down_weight_kernel,
        grid_spec=pltpu.PrefetchScalarGridSpec(
            num_scalar_prefetch=1,
            grid=(8,),
            in_specs=[pl.BlockSpec((slots, units), lambda i, owner: (0, 0))]
            + [whole] * 4
            + [pl.BlockSpec((slots, size), lambda i, owner: (0, jnp.maximum(i - 4, 0)))],
            out_specs=pl.BlockSpec((units, size), out_block),
        ),
        out_shape=jax.ShapeDtypeStruct((units, 8 * size), bf16),
        cost_estimate=light,
        compiler_params=pltpu.CompilerParams(vmem_limit_bytes=40 << 20),
        name="down_weight_grads",
    )(owners, hid, *parts)


def route(group_logits, expert_logits, expert_ids, capacity):
    rows, groups = group_logits.shape
    experts = expert_logits.shape[1]
    per = experts // groups
    group_probs = jax.nn.softmax(group_logits.T, axis=0)
    inner = jax.nn.softmax(expert_logits.T.reshape(groups, per, rows), axis=1)
    gate = route_scale * group_probs[:, None, :] * inner
    ids = expert_ids.T
    numbers = jnp.arange(experts, dtype=jnp.int32)
    chosen = jnp.any(ids[:, None, :] == numbers[None, :, None], axis=0)
    earlier = jnp.arange(rows)[:, None] < jnp.arange(rows)[None, :]
    rank = dot(chosen.astype(bf16), earlier.astype(bf16))
    code = jnp.where(chosen, rank, -1.0).astype(bf16)
    slots = experts * capacity
    spread = (jnp.arange(slots)[:, None] // capacity == numbers[None, :]).astype(bf16)
    place = (jnp.arange(slots) % capacity).astype(f32)[:, None]
    pick = dot(spread, code) == place
    gate_half = gate.astype(bf16).reshape(experts, rows)
    slot_gate = jnp.sum(jnp.where(pick, dot(spread, gate_half), 0.0), axis=1)
    return group_probs, inner, pick.astype(bf16), spread, slot_gate


def with_lanes(value, extra):
    pad = jnp.zeros((value.shape[0], 128 - len(extra)), bf16)
    return jnp.concatenate([value, *extra, pad], axis=1)


def body(tokens, cotangent, group_logits, expert_logits, expert_ids, w_gate, w_up, w_down):
    rows, width = tokens.shape
    experts = expert_logits.shape[1]
    groups = group_logits.shape[1]
    capacity = min(rows, (rows * expert_ids.shape[1] + experts - 1) // experts + 2)
    slots = experts * capacity
    half = slots // 2
    w_gate, w_up, w_down = w_gate[0], w_up[0], w_down[0]
    units = w_down.shape[0]
    me = lax.axis_index("tp")
    far, right, left = (me + 2) % 4, (me + 1) % 4, (me + 3) % 4

    def columns(owner):
        return lax.dynamic_slice(w_down, (0, owner * width), (units, width))

    blocks = [columns(owner) for owner in (me, right, left, far)]
    tokens, *blocks = tie(tokens, *blocks)
    down_own = blocks[0]
    down_left, down_right, down_far = up(blocks[1]), down(blocks[2]), across(blocks[3])

    owners = jnp.stack([me, left, right, far]).astype(jnp.int32)
    cut = width // 2
    share = cotangent[:, cut:]
    ahead = jnp.concatenate([share, up(share), down(share), across(share)], axis=1)
    wide = jnp.concatenate([w_gate, w_up], axis=1)
    down_ahead = jnp.concatenate(
        [
            lax.dynamic_slice(w_down, (0, owner * width + cut), (units, cut))
            for owner in (me, left, right, far)
        ],
        axis=1,
    )
    group_probs, inner, pick, spread, slot_gate = route(
        group_logits, expert_logits, expert_ids, capacity
    )
    lane = jnp.arange(128)[None, :]
    spare = jnp.zeros((rows, 128), bf16)
    tok = exchange(dot(pick, tokens).astype(bf16).reshape(experts, capacity, width))
    sent = dot(pick, jnp.concatenate([cotangent[:, :cut], spare], axis=1))
    at_lane = jnp.arange(cut + 128)[None, :] == cut
    sent = jnp.where(at_lane, slot_gate[:, None], sent).astype(bf16)
    sent = sent.reshape(experts, capacity, -1)
    ahead = dot(pick, ahead).astype(bf16).reshape(experts, capacity, -1)
    sent, wide, down_ahead, ahead, down_left, down_right, down_far = tie(
        sent, wide, down_ahead, ahead, down_left, down_right, down_far
    )
    cot = exchange(sent)
    cot, ahead = tie(cot, ahead)
    ahead = exchange(ahead)
    gate = cot[:, :, cut : cut + 1].reshape(slots, 1).astype(f32)
    cot = cot[:, :, :cut].reshape(slots, cut)
    tok = tok.reshape(slots, width)

    def gather(value, far_first=None):
        from_left, from_right = up(value), down(value)
        return from_left, from_right, up(from_left[:half]), down(from_right[half:])

    tok_left, tok_right, *tok_far = gather(tok)
    *tok_far, cot = tie(*tok_far, cot)
    tok_far = jnp.concatenate(tok_far, axis=0)
    pieces = ((tok, me), (tok_left, left), (tok_right, right), (tok_far, far))

    cot_left, cot_right, *cot_far = gather(cot)
    ahead = ahead.reshape(slots, -1)
    back = dot(ahead, down_ahead, ((1,), (1,)))
    *cot_far, back = tie(*cot_far, back)
    cots = (cot, cot_left, cot_right, jnp.concatenate(cot_far, axis=0))

    def rows_of(owner, lo, size):
        return lax.dynamic_slice(wide, (owner * width + lo, 0), (size, 2 * units))

    last = ((1,), (1,))
    pre = dot(tok, rows_of(me, 0, width))
    for part, owner in pieces[1:]:
        pre = pre + dot(part, rows_of(owner, 0, width))
    pre_gate, pre_up = pre[:, :units], pre[:, units:]

    sig = jax.nn.sigmoid(pre_gate)
    silu = pre_gate * sig
    hidden = silu * pre_up
    weighted = (hidden * gate).astype(bf16)
    weighted, cot_far = tie(weighted, cots[3])
    cots = (*cots[:3], cot_far)
    hid_left = up(weighted)
    hid_right = down(weighted)
    hid_far = across(weighted)
    hids = (weighted, hid_left, hid_right, hid_far)
    downs = (down_own, down_left, down_right, down_far)

    for part, owner in zip(cots, (me, left, right, far)):
        back = back + dot(part, lax.dynamic_slice(w_down, (0, owner * width), (units, cut)), last)

    gate_grad = jnp.sum(hidden * back, axis=1)
    back = back * gate
    grad_gate = (back * pre_up * sig * (1.0 + pre_gate * (1.0 - sig))).astype(bf16)
    grad_up = (back * silu).astype(bf16)
    grads = jnp.concatenate([grad_gate, grad_up], axis=1)

    def grad_part(owner, lo, size):
        return dot(grads, rows_of(owner, lo, size), last)

    spans = ((0, 768), (768, 512))
    firsts = [grad_part(far, *span).astype(bf16) for span in spans]
    *firsts, weighted, hid_left, hid_right, hid_far = tie(*firsts, *hids)
    hids = (weighted, hid_left, hid_right, hid_far)
    news = [(up(part[:half]), down(part[half:])) for part in firsts]
    (one, two), (three, four) = news
    one, two, three, four = tie(one, two, three, four)
    news = (one, two), (three, four)
    out = sum(dot(h, d) for h, d in zip(hids, downs))
    high = lax.reduce_precision(gate_grad, 8, 7)
    low = lax.reduce_precision(gate_grad - high, 8, 7)
    side = jnp.where(lane == 0, high[:, None], jnp.where(lane == 1, low[:, None], 0.0))
    out = jnp.concatenate([out.astype(bf16), side.astype(bf16)], axis=1)
    out = exchange(out.reshape(experts, capacity, -1))

    sums = []
    for span, (from_left, from_right) in zip(spans, news):
        toward, away = grad_part(right, *span), grad_part(left, *span)
        toward = jnp.concatenate([toward[:half] + from_left.astype(f32), toward[half:]], axis=0)
        away = jnp.concatenate([away[:half], away[half:] + from_right.astype(f32)], axis=0)
        toward, away = toward.astype(bf16), away.astype(bf16)
        if sums:
            toward, away, *sums[0] = tie(toward, away, *sums[0])
        sums.append([up(toward), down(away)])
    totals = [
        (grad_part(me, *span) + one.astype(f32) + two.astype(f32)).astype(bf16)
        for span, (one, two) in zip(spans, sums)
    ]
    totals = [total.reshape(experts, capacity, -1) for total in totals]
    out, totals[0], grads, weighted = tie(out, totals[0], grads, weighted)
    lead = exchange(totals[0])
    lead, totals[1] = tie(lead, totals[1])
    gate_grad = out[:, :, width:].reshape(slots, 128)[:, :2]
    gate_grad = jnp.sum(gate_grad.astype(f32), axis=1, keepdims=True)
    mixed = dot(pick, out[:, :, :width].reshape(slots, width), outer).astype(bf16)

    tail = exchange(totals[1])
    token_grad = jnp.concatenate(
        [dot(pick, part.reshape(slots, -1), outer).astype(bf16) for part in (lead, tail)], axis=1
    )

    d_gate, d_up = up_weight_grads(owners, [part for part, _ in pieces], grads)
    d_down = down_weight_grads(owners, weighted, [*cots, ahead])

    dense = lax.dot_general(
        spread.astype(f32) * gate_grad, pick.astype(f32), (outer, ((), ())),
        precision=lax.Precision.HIGHEST, preferred_element_type=f32,
    )
    dense = dense + up(dense) + down(dense) + across(dense)
    dense = dense.reshape(groups, experts // groups, rows)
    scaled = route_scale * dense * inner
    group_part = jnp.sum(scaled, axis=1)
    group_grad = group_probs * (group_part - jnp.sum(group_probs * group_part, axis=0, keepdims=True))
    logit_grad = group_probs[:, None, :] * (scaled - inner * group_part[:, None, :])
    return (
        mixed,
        token_grad,
        group_grad.T,
        logit_grad.reshape(experts, rows).T,
        d_gate[None],
        d_up[None],
        d_down[None],
    )


def solution(mesh):
    rows = P(both, "tp")
    router = P(both, None)
    wide = P(both, None, "tp")
    tall = P(both, "tp", None)
    return jax.shard_map(
        body,
        mesh=mesh,
        in_specs=(rows, rows, router, router, router, wide, wide, tall),
        out_specs=(rows, rows, router, router, wide, wide, tall),
        check_vma=False,
    )
```

```python
import jax
import jax.numpy as jnp
from jax import lax
from jax.experimental import pallas as pl
from jax.experimental.pallas import tpu as pltpu
from jax.sharding import PartitionSpec as P

route_scale = 16.0
both = ("group", "expert")
bf16 = jnp.bfloat16
f32 = jnp.float32


def dot(left, right, dims=((1,), (0,))):
    return lax.dot_general(left, right, (dims, ((), ())), preferred_element_type=f32)


def up(value):
    return lax.ppermute(value, "tp", [(i, (i + 1) % 4) for i in range(4)])


def down(value):
    return lax.ppermute(value, "tp", [(i, (i + 3) % 4) for i in range(4)])


def across(value):
    return lax.ppermute(value, "tp", [(i, (i + 2) % 4) for i in range(4)])


def tie(*values):
    return lax.optimization_barrier(values)


def exchange(value):
    return lax.all_to_all(value, both, split_axis=0, concat_axis=0, tiled=True)


light = pl.CostEstimate(flops=1, bytes_accessed=1, transcendentals=0)
outer = ((0,), (0,))


def up_weight_kernel(owner_ref, own, left, right, far, grad_ref, gate_ref, up_ref):
    step = pl.program_id(0)
    for number, part in enumerate((own, left, right, far)):

        @pl.when(step // 2 == number)
        def _():
            both_grads = dot(part[...], grad_ref[...], outer).astype(bf16)
            units = gate_ref.shape[1]
            gate_ref[...] = both_grads[:, :units]
            up_ref[...] = both_grads[:, units:]


def up_weight_grads(owners, parts, grads):
    slots, width = parts[0].shape
    units = grads.shape[1] // 2
    size = width // 2

    def part_spec(number):
        return pl.BlockSpec(
            (slots, size), lambda i, owner: (0, jnp.clip(i - 2 * number, 0, 1))
        )

    out_spec = pl.BlockSpec((size, units), lambda i, owner: (owner[i // 2] * 2 + i % 2, 0))
    shape = jax.ShapeDtypeStruct((4 * width, units), bf16)
    return pl.pallas_call(
        up_weight_kernel,
        grid_spec=pltpu.PrefetchScalarGridSpec(
            num_scalar_prefetch=1,
            grid=(8,),
            in_specs=[part_spec(n) for n in range(4)]
            + [pl.BlockSpec((slots, 2 * units), lambda i, owner: (0, 0))],
            out_specs=[out_spec, out_spec],
        ),
        out_shape=[shape, shape],
        cost_estimate=light,
        compiler_params=pltpu.CompilerParams(vmem_limit_bytes=40 << 20),
        name="up_weight_grads",
    )(owners, *parts, grads)


def down_weight_kernel(owner_ref, hid_ref, tall_ref, *refs):
    *parts, ahead, out_ref = refs
    size, rest = parts[0].shape[1], ahead.shape[1] // 4
    for number, part in enumerate(parts):
        at = pl.multiple_of(owner_ref[number] * (size + rest), 128)
        out_ref[:, pl.ds(at, size)] = dot(hid_ref[...], part[...], outer).astype(bf16)

    @pl.loop(0, 4)
    def _(number):
        at = pl.multiple_of(owner_ref[number] * (size + rest) + size, 128)
        block = ahead[:, pl.ds(pl.multiple_of(number * rest, 128), rest)]
        out_ref[:, pl.ds(at, rest)] = dot(tall_ref[...], block, outer).astype(bf16)


def down_weight_grads(owners, hid, tall, parts, ahead):
    units = hid.shape[1]
    width = 4 * parts[0].shape[1] + ahead.shape[1]
    operands = (hid, tall, *parts, ahead)
    return pl.pallas_call(
        down_weight_kernel,
        grid_spec=pltpu.PrefetchScalarGridSpec(
            num_scalar_prefetch=1,
            grid=(1,),
            in_specs=[pl.BlockSpec(x.shape, lambda i, owner: (0, 0)) for x in operands],
            out_specs=pl.BlockSpec((units, width), lambda i, owner: (0, 0)),
        ),
        out_shape=jax.ShapeDtypeStruct((units, width), bf16),
        cost_estimate=light,
        compiler_params=pltpu.CompilerParams(vmem_limit_bytes=48 << 20),
        name="down_weight_grads",
    )(owners, *operands)


def route(group_logits, expert_logits, expert_ids, block):
    rows, groups = group_logits.shape
    experts = expert_logits.shape[1]
    per = experts // groups
    group_probs = jax.nn.softmax(group_logits.T, axis=0)
    inner = jax.nn.softmax(expert_logits.T.reshape(groups, per, rows), axis=1)
    gate = route_scale * group_probs[:, None, :] * inner
    ids = expert_ids.T
    numbers = jnp.arange(experts, dtype=jnp.int32)
    chosen = jnp.any(ids[:, None, :] == numbers[None, :, None], axis=0)
    earlier = jnp.arange(rows)[:, None] < jnp.arange(rows)[None, :]
    rank = dot(chosen.astype(bf16), earlier.astype(bf16))
    code = jnp.where(chosen, rank, -1.0).astype(bf16)
    slots = experts * block
    spread = (jnp.arange(slots)[:, None] // block == numbers[None, :]).astype(bf16)
    place = (jnp.arange(slots) % block).astype(f32)[:, None]
    pick = dot(spread, code) == place
    gate_half = gate.astype(bf16).reshape(experts, rows)
    slot_gate = jnp.sum(jnp.where(pick, dot(spread, gate_half), 0.0), axis=1)
    return group_probs, inner, pick.astype(bf16), spread, slot_gate


def with_lanes(value, extra):
    pad = jnp.zeros((value.shape[0], 128 - len(extra)), bf16)
    return jnp.concatenate([value, *extra, pad], axis=1)


def body(tokens, cotangent, group_logits, expert_logits, expert_ids, w_gate, w_up, w_down):
    rows, width = tokens.shape
    experts = expert_logits.shape[1]
    groups = group_logits.shape[1]
    capacity = min(rows, (rows * expert_ids.shape[1] + experts - 1) // experts + 2)
    slots = experts * capacity
    half = slots // 2
    block = (capacity + 15) // 16 * 16

    def blocks_of(value):
        value = value.reshape(experts, capacity, -1)
        return jnp.pad(value, ((0, 0), (0, block - capacity), (0, 0)))

    def slots_of(value):
        return value.reshape(experts, block, -1)[:, :capacity].reshape(slots, -1)

    w_gate, w_up, w_down = w_gate[0], w_up[0], w_down[0]
    units = w_down.shape[0]
    me = lax.axis_index("tp")
    far, right, left = (me + 2) % 4, (me + 1) % 4, (me + 3) % 4

    def columns(owner):
        return lax.dynamic_slice(w_down, (0, owner * width), (units, width))

    blocks = [columns(owner) for owner in (me, right, left, far)]
    cut = 2 * (width // 5)
    share = cotangent[:, cut:]
    ahead = jnp.concatenate([share, up(share), down(share), across(share)], axis=1)
    down_own = blocks[0]
    down_left, down_right, down_far = up(blocks[1]), down(blocks[2]), across(blocks[3])

    owners = jnp.stack([me, left, right, far]).astype(jnp.int32)
    wide = jnp.concatenate([w_gate, w_up], axis=1)
    down_ahead = jnp.concatenate(
        [
            lax.dynamic_slice(w_down, (0, owner * width + cut), (units, width - cut))
            for owner in (me, left, right, far)
        ],
        axis=1,
    )
    group_probs, inner, pick, spread, slot_gate = route(
        group_logits, expert_logits, expert_ids, block
    )
    lane = jnp.arange(128)[None, :]
    spare = jnp.zeros((rows, 128), bf16)
    sent = dot(pick, jnp.concatenate([tokens, cotangent[:, :cut], spare], axis=1))
    at_lane = jnp.arange(sent.shape[1])[None, :] == width + cut
    sent = jnp.where(at_lane, slot_gate[:, None], sent).astype(bf16)
    sent, ahead = tie(sent.reshape(experts, block, -1), ahead)
    sent = exchange(sent)
    ahead = dot(pick, ahead).astype(bf16).reshape(experts, block, -1)
    tok = slots_of(sent[:, :, :width])

    def rows_of(owner, lo, size):
        return lax.dynamic_slice(wide, (owner * width + lo, 0), (size, 2 * units))

    tok, wide, down_ahead, ahead, down_left, down_right, down_far = tie(
        tok, wide, down_ahead, ahead, down_left, down_right, down_far
    )
    ahead = exchange(ahead)
    pre = dot(tok, rows_of(me, 0, width))
    cot = slots_of(sent[:, :, width : width + cut])
    gate = slots_of(sent[:, :, width + cut : width + cut + 1]).astype(f32)

    def gather(value):
        from_left, from_right = up(value), down(value)
        return from_left, from_right, up(from_left[:half]), down(from_right[half:])

    tok_left, tok_right, *tok_far = gather(tok)
    *tok_far, cot = tie(*tok_far, cot)
    tok_far = jnp.concatenate(tok_far, axis=0)
    pieces = ((tok, me), (tok_left, left), (tok_right, right), (tok_far, far))

    cot_left, cot_right, *cot_far = gather(cot)
    ahead = ahead.reshape(experts * block, -1)
    back = slots_of(dot(ahead, down_ahead, ((1,), (1,))))
    *cot_far, back = tie(*cot_far, back)
    cots = (cot, cot_left, cot_right, jnp.concatenate(cot_far, axis=0))

    last = ((1,), (1,))
    for part, owner in pieces[1:]:
        pre = pre + dot(part, rows_of(owner, 0, width))
    pre_gate, pre_up = pre[:, :units], pre[:, units:]

    sig = jax.nn.sigmoid(pre_gate)
    silu = pre_gate * sig
    hidden = silu * pre_up
    weighted = (hidden * gate).astype(bf16)
    weighted, cot_far = tie(weighted, cots[3])
    cots = (*cots[:3], cot_far)
    hid_left = up(weighted)
    hid_right = down(weighted)
    hid_far = across(weighted)
    hids = (weighted, hid_left, hid_right, hid_far)
    downs = (down_own, down_left, down_right, down_far)

    for part, owner in zip(cots, (me, left, right, far)):
        back = back + dot(part, lax.dynamic_slice(w_down, (0, owner * width), (units, cut)), last)

    gate_grad = jnp.sum(hidden * back, axis=1)
    back = back * gate
    grad_gate = (back * pre_up * sig * (1.0 + pre_gate * (1.0 - sig))).astype(bf16)
    grad_up = (back * silu).astype(bf16)
    grads = jnp.concatenate([grad_gate, grad_up], axis=1)

    def grad_part(owner, lo, size):
        return dot(grads, rows_of(owner, lo, size), last)

    part = grad_part(far, 0, width).astype(bf16)
    from_left, from_right = up(part[:half]), down(part[half:])

    out = sum(dot(h, d) for h, d in zip(hids, downs))
    high = lax.reduce_precision(gate_grad, 8, 7)
    low = lax.reduce_precision(gate_grad - high, 8, 7)
    side = jnp.where(lane == 0, high[:, None], jnp.where(lane == 1, low[:, None], 0.0))
    out = jnp.concatenate([out.astype(bf16), side.astype(bf16)], axis=1)
    out = out.reshape(experts, capacity, -1)
    toward, away = grad_part(right, 0, width), grad_part(left, 0, width)
    toward, away, out = tie(toward, away, out)
    out = exchange(out)

    toward = jnp.concatenate([toward[:half] + from_left.astype(f32), toward[half:]], axis=0)
    away = jnp.concatenate([away[:half], away[half:] + from_right.astype(f32)], axis=0)
    split = 3 * (width // 5)
    spans = ((0, split), (split, width - split))
    sends = []
    for lo, size in spans:
        sends += [toward[:, lo : lo + size].astype(bf16), away[:, lo : lo + size].astype(bf16)]
    *sends, grads, weighted = tie(*sends, grads, weighted)
    sums = [(up(sends[0]), down(sends[1])), (up(sends[2]), down(sends[3]))]
    d_gate, d_up = up_weight_grads(owners, [part for part, _ in pieces], grads)
    one, two, d_gate, d_up = tie(*sums[0], d_gate, d_up)
    sums[0] = one, two
    totals = [
        (grad_part(me, *span) + one.astype(f32) + two.astype(f32)).astype(bf16)
        for span, (one, two) in zip(spans, sums)
    ]
    totals = [total.reshape(experts, capacity, -1) for total in totals]
    pick, spread = slots_of(pick), slots_of(spread)
    out, totals[0] = tie(out, totals[0])
    lead, totals[1], weighted = tie(exchange(totals[0]), totals[1], weighted)
    tail = exchange(totals[1])
    d_down = down_weight_grads(
        owners, weighted, blocks_of(weighted).reshape(experts * block, -1), cots, ahead
    )
    gate_grad = out[:, :, width:].reshape(slots, 128)[:, :2]
    gate_grad = jnp.sum(gate_grad.astype(f32), axis=1, keepdims=True)
    mixed = dot(pick, out[:, :, :width].reshape(slots, width), outer).astype(bf16)

    token_grad = jnp.concatenate(
        [dot(pick, part.reshape(slots, -1), outer).astype(bf16) for part in (lead, tail)], axis=1
    )

    dense = lax.dot_general(
        spread.astype(f32) * gate_grad, pick.astype(f32), (outer, ((), ())),
        precision=lax.Precision.HIGHEST, preferred_element_type=f32,
    )
    dense = dense + up(dense) + down(dense) + across(dense)
    dense = dense.reshape(groups, experts // groups, rows)
    scaled = route_scale * dense * inner
    group_part = jnp.sum(scaled, axis=1)
    group_grad = group_probs * (group_part - jnp.sum(group_probs * group_part, axis=0, keepdims=True))
    logit_grad = group_probs[:, None, :] * (scaled - inner * group_part[:, None, :])
    return (
        mixed,
        token_grad,
        group_grad.T,
        logit_grad.reshape(experts, rows).T,
        d_gate[None],
        d_up[None],
        d_down[None],
    )


def solution(mesh):
    rows = P(both, "tp")
    router = P(both, None)
    wide = P(both, None, "tp")
    tall = P(both, "tp", None)
    return jax.shard_map(
        body,
        mesh=mesh,
        in_specs=(rows, rows, router, router, router, wide, wide, tall),
        out_specs=(rows, rows, router, router, wide, wide, tall),
        check_vma=False,
    )
```

```python
import functools

import jax
import jax.numpy as jnp
from jax import lax
from jax.experimental import pallas as pl
from jax.experimental.pallas import tpu as pltpu
from jax.sharding import PartitionSpec as P

route_scale = 16.0
both = ("group", "expert")
bf16 = jnp.bfloat16
f32 = jnp.float32


def dot(left, right, dims=((1,), (0,))):
    return lax.dot_general(left, right, (dims, ((), ())), preferred_element_type=f32)


def up(value):
    return lax.ppermute(value, "tp", [(i, (i + 1) % 4) for i in range(4)])


def down(value):
    return lax.ppermute(value, "tp", [(i, (i + 3) % 4) for i in range(4)])


def across(value):
    return lax.ppermute(value, "tp", [(i, (i + 2) % 4) for i in range(4)])


def tie(*values):
    return lax.optimization_barrier(values)


def exchange(value):
    return lax.all_to_all(value, both, split_axis=0, concat_axis=0, tiled=True)


light = pl.CostEstimate(flops=1, bytes_accessed=1, transcendentals=0)
outer = ((0,), (0,))


def up_weight_kernel(owner_ref, own, left, right, far, grad_ref, gate_ref, up_ref):
    step = pl.program_id(0)
    for number, part in enumerate((own, left, right, far)):

        @pl.when(step // 2 == number)
        def _():
            both_grads = dot(part[...], grad_ref[...], outer).astype(bf16)
            units = gate_ref.shape[1]
            gate_ref[...] = both_grads[:, :units]
            up_ref[...] = both_grads[:, units:]


def up_weight_grads(owners, parts, grads):
    slots, width = parts[0].shape
    units = grads.shape[1] // 2
    size = width // 2

    def part_spec(number):
        return pl.BlockSpec(
            (slots, size), lambda i, owner: (0, jnp.clip(i - 2 * number, 0, 1))
        )

    out_spec = pl.BlockSpec((size, units), lambda i, owner: (owner[i // 2] * 2 + i % 2, 0))
    shape = jax.ShapeDtypeStruct((4 * width, units), bf16)
    return pl.pallas_call(
        up_weight_kernel,
        grid_spec=pltpu.PrefetchScalarGridSpec(
            num_scalar_prefetch=1,
            grid=(8,),
            in_specs=[part_spec(n) for n in range(4)]
            + [pl.BlockSpec((slots, 2 * units), lambda i, owner: (0, 0))],
            out_specs=[out_spec, out_spec],
        ),
        out_shape=[shape, shape],
        cost_estimate=light,
        compiler_params=pltpu.CompilerParams(vmem_limit_bytes=40 << 20),
        name="up_weight_grads",
    )(owners, *parts, grads)


def down_weight_kernel(owner_ref, hid_ref, tall_ref, *refs):
    *parts, ahead, out_ref = refs
    size, rest = parts[0].shape[1], ahead.shape[1] // 4
    for number, part in enumerate(parts):
        at = pl.multiple_of(owner_ref[number] * (size + rest), 128)
        out_ref[:, pl.ds(at, size)] = dot(hid_ref[...], part[...], outer).astype(bf16)

    @pl.loop(0, 4)
    def _(number):
        at = pl.multiple_of(owner_ref[number] * (size + rest) + size, 128)
        block = ahead[:, pl.ds(pl.multiple_of(number * rest, 128), rest)]
        out_ref[:, pl.ds(at, rest)] = dot(tall_ref[...], block, outer).astype(bf16)


def down_weight_grads(owners, hid, tall, parts, ahead):
    units = hid.shape[1]
    width = 4 * parts[0].shape[1] + ahead.shape[1]
    operands = (hid, tall, *parts, ahead)
    return pl.pallas_call(
        down_weight_kernel,
        grid_spec=pltpu.PrefetchScalarGridSpec(
            num_scalar_prefetch=1,
            grid=(1,),
            in_specs=[pl.BlockSpec(x.shape, lambda i, owner: (0, 0)) for x in operands],
            out_specs=pl.BlockSpec((units, width), lambda i, owner: (0, 0)),
        ),
        out_shape=jax.ShapeDtypeStruct((units, width), bf16),
        cost_estimate=light,
        compiler_params=pltpu.CompilerParams(vmem_limit_bytes=48 << 20),
        name="down_weight_grads",
    )(owners, *operands)


def page_kernel(dots, adds, capacity, *refs):
    lefts, rights = refs[:dots], refs[dots : 2 * dots]
    terms = refs[2 * dots : 2 * dots + adds]
    side_ref, out_ref, acc, page = refs[2 * dots + adds :]
    total = terms[0][...].astype(f32)
    for term in terms[1:]:
        total += term[...].astype(f32)
    for left, right in zip(lefts, rights):
        total += dot(left[...], right[...])
    acc[...] = total
    columns = page.shape[1]
    for e in range(out_ref.shape[0]):
        lines = acc[e * capacity : (e + 1) * capacity, :]
        page[:capacity, :] = lines[:, :columns]
        page[capacity : 2 * capacity, :] = lines[:, columns:]
        page[2 * capacity :, :] = side_ref[e]
        out_ref[e] = page[...].astype(bf16)


def paged(lefts, rights, terms, side, capacity):
    slots, width = terms[0].shape
    experts, spare, columns = side.shape
    part, lines = slots // 2, 2 * capacity + spare

    def half_of(shape):
        return pl.BlockSpec((shape[0] // 2, *shape[1:]), lambda i: (i,) + (0,) * (len(shape) - 1))

    return pl.pallas_call(
        functools.partial(page_kernel, len(lefts), len(terms), capacity),
        grid=(2,),
        in_specs=[half_of(x.shape) for x in lefts]
        + [pl.BlockSpec(x.shape, lambda i: (0, 0)) for x in rights]
        + [half_of(x.shape) for x in (*terms, side)],
        out_specs=half_of((experts, lines, columns)),
        out_shape=jax.ShapeDtypeStruct((experts, lines, columns), bf16),
        scratch_shapes=[pltpu.VMEM((part, width), f32), pltpu.VMEM((lines, columns), f32)],
        cost_estimate=pl.CostEstimate(
            flops=sum(2 * slots * x.shape[0] * width for x in rights),
            bytes_accessed=12 * slots * width,
            transcendentals=0,
        ),
        compiler_params=pltpu.CompilerParams(vmem_limit_bytes=48 << 20),
        name="pages",
    )(*lefts, *rights, *terms, side)


def route(group_logits, expert_logits, expert_ids, capacity, block, lines):
    rows, groups = group_logits.shape
    experts = expert_logits.shape[1]
    per = experts // groups
    group_probs = jax.nn.softmax(group_logits.T, axis=0)
    inner = jax.nn.softmax(expert_logits.T.reshape(groups, per, rows), axis=1)
    gate = route_scale * group_probs[:, None, :] * inner
    ids = expert_ids.T
    numbers = jnp.arange(experts, dtype=jnp.int32)
    chosen = jnp.any(ids[:, None, :] == numbers[None, :, None], axis=0)
    earlier = jnp.arange(rows)[:, None] < jnp.arange(rows)[None, :]
    rank = dot(chosen.astype(bf16), earlier.astype(bf16))
    code = jnp.where(chosen, rank, -1.0).astype(bf16)
    slots = experts * block
    spread = (jnp.arange(slots)[:, None] // block == numbers[None, :]).astype(bf16)
    place = (jnp.arange(slots) % block).astype(f32)[:, None]
    pick = dot(spread, code) == place
    gate_half = gate.astype(bf16).reshape(experts, rows)
    slot_gate = jnp.sum(jnp.where(pick, dot(spread, gate_half), 0.0), axis=1)
    row = jnp.arange(experts * lines)
    code_rows = dot((row[:, None] // lines == numbers[None, :]).astype(bf16), code)
    page_picks = []
    for part in range(2):
        at = row % lines - part * capacity
        at = jnp.where((at >= 0) & (at < capacity), at, -2).astype(f32)
        page_picks.append((code_rows == at[:, None]).astype(bf16))
    return group_probs, inner, pick.astype(bf16), page_picks, spread, slot_gate


def with_lanes(value, extra):
    pad = jnp.zeros((value.shape[0], 128 - len(extra)), bf16)
    return jnp.concatenate([value, *extra, pad], axis=1)


def body(tokens, cotangent, group_logits, expert_logits, expert_ids, w_gate, w_up, w_down):
    rows, width = tokens.shape
    experts = expert_logits.shape[1]
    groups = group_logits.shape[1]
    capacity = min(rows, (rows * expert_ids.shape[1] + experts - 1) // experts + 2)
    slots = experts * capacity
    half = slots // 2
    block = (capacity + 15) // 16 * 16
    lines = (2 * capacity + 9) // 8 * 8

    def blocks_of(value):
        value = value.reshape(experts, capacity, -1)
        return jnp.pad(value, ((0, 0), (0, block - capacity), (0, 0)))

    def slots_of(value):
        return value.reshape(experts, block, -1)[:, :capacity].reshape(slots, -1)

    w_gate, w_up, w_down = w_gate[0], w_up[0], w_down[0]
    units = w_down.shape[0]
    me = lax.axis_index("tp")
    far, right, left = (me + 2) % 4, (me + 1) % 4, (me + 3) % 4

    def columns(owner):
        return lax.dynamic_slice(w_down, (0, owner * width), (units, width))

    blocks = [columns(owner) for owner in (me, right, left, far)]
    cut = 2 * (width // 5)
    share = cotangent[:, cut:]
    ahead = jnp.concatenate([share, up(share), down(share), across(share)], axis=1)
    down_own = blocks[0]
    down_left, down_right, down_far = up(blocks[1]), down(blocks[2]), across(blocks[3])

    owners = jnp.stack([me, left, right, far]).astype(jnp.int32)
    wide = jnp.concatenate([w_gate, w_up], axis=1)
    down_ahead = jnp.concatenate(
        [
            lax.dynamic_slice(w_down, (0, owner * width + cut), (units, width - cut))
            for owner in (me, left, right, far)
        ],
        axis=1,
    )
    group_probs, inner, pick, page_picks, spread, slot_gate = route(
        group_logits, expert_logits, expert_ids, capacity, block, lines
    )
    lane = jnp.arange(128)[None, :]
    spare = jnp.zeros((rows, 128), bf16)
    sent = dot(pick, jnp.concatenate([tokens, cotangent[:, :cut], spare], axis=1))
    at_lane = jnp.arange(sent.shape[1])[None, :] == width + cut
    sent = jnp.where(at_lane, slot_gate[:, None], sent).astype(bf16)
    sent, ahead = tie(sent.reshape(experts, block, -1), ahead)
    sent = exchange(sent)
    ahead = dot(pick, ahead).astype(bf16).reshape(experts, block, -1)
    tok = slots_of(sent[:, :, :width])

    def rows_of(owner, lo, size):
        return lax.dynamic_slice(wide, (owner * width + lo, 0), (size, 2 * units))

    tok, wide, down_ahead, ahead, down_left, down_right, down_far = tie(
        tok, wide, down_ahead, ahead, down_left, down_right, down_far
    )
    ahead = exchange(ahead)
    pre = dot(tok, rows_of(me, 0, width))
    cot = slots_of(sent[:, :, width : width + cut])
    gate = slots_of(sent[:, :, width + cut : width + cut + 1]).astype(f32)

    def gather(value):
        from_left, from_right = up(value), down(value)
        return from_left, from_right, up(from_left[:half]), down(from_right[half:])

    tok_left, tok_right, *tok_far = gather(tok)
    *tok_far, cot = tie(*tok_far, cot)
    tok_far = jnp.concatenate(tok_far, axis=0)
    pieces = ((tok, me), (tok_left, left), (tok_right, right), (tok_far, far))

    cot_left, cot_right, *cot_far = gather(cot)
    ahead = ahead.reshape(experts * block, -1)
    back = slots_of(dot(ahead, down_ahead, ((1,), (1,))))
    cots = (cot, cot_left, cot_right, jnp.concatenate(cot_far, axis=0))

    last = ((1,), (1,))
    for part, owner in pieces[1:]:
        pre = pre + dot(part, rows_of(owner, 0, width))
    pre_gate, pre_up = pre[:, :units], pre[:, units:]

    sig = jax.nn.sigmoid(pre_gate)
    silu = pre_gate * sig
    hidden = silu * pre_up
    weighted = (hidden * gate).astype(bf16)
    weighted, cot_far = tie(weighted, cots[3])
    cots = (*cots[:3], cot_far)
    hid_left = up(weighted)
    hid_right = down(weighted)
    hid_far = across(weighted)
    hids = [weighted, hid_left, hid_right, hid_far]
    downs = (down_own, down_left, down_right, down_far)

    for part, owner in zip(cots, (me, left, right, far)):
        back = back + dot(part, lax.dynamic_slice(w_down, (0, owner * width), (units, cut)), last)

    gate_grad = jnp.sum(hidden * back, axis=1)
    back = back * gate
    grad_gate = (back * pre_up * sig * (1.0 + pre_gate * (1.0 - sig))).astype(bf16)
    grad_up = (back * silu).astype(bf16)
    grads = jnp.concatenate([grad_gate, grad_up], axis=1)

    def grad_part(owner, lo, size):
        return dot(grads, rows_of(owner, lo, size), last)

    part = grad_part(far, 0, width).astype(bf16)
    part, *hids[1:] = tie(part, *hids[1:])
    from_left, from_right = up(part[:half]), down(part[half:])

    high = lax.reduce_precision(gate_grad, 8, 7)
    low = lax.reduce_precision(gate_grad - high, 8, 7)
    side = jnp.stack([high.reshape(experts, capacity), low.reshape(experts, capacity)], axis=1)
    side = jnp.pad(side, ((0, 0), (0, lines - 2 * capacity - 2), (0, width // 2 - capacity)))
    out = paged(hids[1:], downs[1:], [dot(weighted, down_own)], side, capacity)
    toward, away = grad_part(right, 0, width), grad_part(left, 0, width)
    toward, out = tie(toward, out)
    out = exchange(out)

    toward = jnp.concatenate([toward[:half] + from_left.astype(f32), toward[half:]], axis=0)
    away = jnp.concatenate([away[:half], away[half:] + from_right.astype(f32)], axis=0)
    split = 3 * (width // 5)
    spans = ((0, split), (split, width - split))
    sends = []
    for lo, size in spans:
        sends += [toward[:, lo : lo + size].astype(bf16), away[:, lo : lo + size].astype(bf16)]
    *sends, grads, weighted = tie(*sends, grads, weighted)
    sums = [(up(sends[0]), down(sends[1])), (up(sends[2]), down(sends[3]))]
    d_gate, d_up = up_weight_grads(owners, [part for part, _ in pieces], grads)
    one, two, d_gate, d_up = tie(*sums[0], d_gate, d_up)
    sums[0] = one, two
    def total_of(span, one, two):
        blank = jnp.zeros((experts, lines - 2 * capacity, span[1] // 2), f32)
        return paged([], [], [grad_part(me, *span), one, two], blank, capacity)

    total = total_of(spans[0], *sums[0])
    out, total = tie(out, total)
    lead, *sums[1] = tie(exchange(total), *sums[1])
    total = total_of(spans[1], *sums[1])
    total, weighted = tie(total, weighted)
    tail = exchange(total)
    d_down = down_weight_grads(
        owners, weighted, blocks_of(weighted).reshape(experts * block, -1), cots, ahead
    )

    gate_grad = jnp.sum(out[:, 2 * capacity : 2 * capacity + 2, :capacity].astype(f32), axis=1)
    gate_grad = jnp.pad(gate_grad, ((0, 0), (0, block - capacity))).reshape(-1, 1)

    def combine(pages):
        pages = pages.reshape(experts * lines, -1)
        return jnp.concatenate([dot(p, pages, outer).astype(bf16) for p in page_picks], axis=1)

    mixed = combine(out)
    token_grad = jnp.concatenate([combine(lead), combine(tail)], axis=1)

    dense = lax.dot_general(
        spread.astype(f32) * gate_grad, pick.astype(f32), (outer, ((), ())),
        precision=lax.Precision.HIGHEST, preferred_element_type=f32,
    )
    dense = dense + up(dense) + down(dense) + across(dense)
    dense = dense.reshape(groups, experts // groups, rows)
    scaled = route_scale * dense * inner
    group_part = jnp.sum(scaled, axis=1)
    group_grad = group_probs * (group_part - jnp.sum(group_probs * group_part, axis=0, keepdims=True))
    logit_grad = group_probs[:, None, :] * (scaled - inner * group_part[:, None, :])
    return (
        mixed,
        token_grad,
        group_grad.T,
        logit_grad.reshape(experts, rows).T,
        d_gate[None],
        d_up[None],
        d_down[None],
    )


def solution(mesh):
    rows = P(both, "tp")
    router = P(both, None)
    wide = P(both, None, "tp")
    tall = P(both, "tp", None)
    return jax.shard_map(
        body,
        mesh=mesh,
        in_specs=(rows, rows, router, router, router, wide, wide, tall),
        out_specs=(rows, rows, router, router, wide, wide, tall),
        check_vma=False,
    )
```
